256 devices in a mesh: mem: 4 (over z_hi), lat: 64 (over x, z_lo, y, core).
Axes of the slice: x: 4, y: 4, z: 8 (z_hi: 4, z_lo: 2; z = z_hi * 2 + z_lo), core: 2. Of those that a mesh axis runs over, the one named last changes fastest.
Arguments:
- members: float32 [32, 2, 512, 1024], P('mem', None, 'lat'), may hold values from -0.75 to 0.75
- lat_root: float32 [512, 512], replicated, may hold values from -1 to 2
- lon_root: float32 [1024, 1024], replicated, may hold values from -1 to 2
- innovation: float32 [512, 256], P('lat', 'mem'), may hold values from -6 to 6
- obs_weight: float32 [512, 256], P('lat', 'mem'), may hold values from 0.5 to 4
- obs_mask: int32 [512, 256], P('lat', 'mem'), may hold values 0 or 1
- obs_cell: int32 [512, 256], P('lat', 'mem'), may hold values from 0 to 2047, as said below
Outputs:
- increment: float32 [2, 512, 1024], P(None, 'lat', 'mem')
- control: float32 [32, 2, 512, 1024], P('mem', None, 'lat')
The draws below stay inside these ranges and needn't reach their ends.
Inputs may be any that keep to these rules, and one draw needn't show every extreme that they name: `obs_cell`: entry e in column c has (e % 1024) // 256 equal to c // 64.
All inputs are finite; a program needn't handle non-finite values. No bound on the sum of `obs_mask` on one device may be relied on, other than what follows from the above.
Results may differ from the reference program's by a relative error of at most 0.0003.
Values sent between devices are 32-bit elements; how exact they have to be, the bound alone decides.
A program may use at most 64 MiB of HBM per device.

```python
import math
import jax
import jax.numpy as jnp
from jax import lax

NLAT = 512
NLON = 1024
LEV = 2
INNER = 2
OBS_ROW = 256
MEMBERS = 32
N_MEM = 4


def root_matrix(key, order):
    noise = jnp.clip(jax.random.normal(key, (order, order), jnp.float32), -4.0, 4.0)
    return jnp.eye(order, dtype=jnp.float32) + 0.5 * noise / math.sqrt(order)


def draw_lat_root(key, part):
    return root_matrix(jax.random.fold_in(key, 11), NLAT)


def draw_lon_root(key, part):
    return root_matrix(jax.random.fold_in(key, 13), NLON)


def draw_obs_cell(key, part):
    per_block = OBS_ROW // N_MEM
    quarter = NLON // N_MEM
    column_block = jnp.arange(OBS_ROW, dtype=jnp.int32) // per_block
    offset = jax.random.randint(jax.random.fold_in(key, 21), (NLAT, OBS_ROW), 0, quarter, dtype=jnp.int32)
    level = jax.random.randint(jax.random.fold_in(key, 23), (NLAT, OBS_ROW), 0, LEV, dtype=jnp.int32)
    return (level * NLON + column_block[None, :] * quarter + offset).astype(jnp.int32)


def plant(drawn, stream_key, low, largest):
    shape = drawn.shape
    place = [jax.random.randint(jax.random.fold_in(stream_key, axis), (), 0, shape[axis]) for axis in range(len(shape))]
    drawn = drawn.at[tuple(place)].set(low)
    longest = shape.index(max(shape))
    place[longest] = (place[longest] + 1) % shape[longest]
    return drawn.at[tuple(place)].set(largest)


def level_of(stream_key, shape, split, smallest, high):
    gain = 1.0
    for position, blocks in split:
        steps = jax.random.uniform(jax.random.fold_in(jax.random.fold_in(stream_key, 6), position), (blocks,), jnp.float32, smallest / len(split), high / len(split))
        gain = gain * jnp.repeat(jnp.exp(steps), shape[position] // blocks).reshape((-1,) + (1,) * (len(shape) - 1 - position))
    return gain


def bell_draw(rng, shape, width, most, pieces=(), kind=jnp.bfloat16):
    gain = level_of(rng, shape, pieces, -0.22, 0.18) if pieces else 1.0
    result = jax.random.normal(rng, shape, jnp.float32) * width * gain
    return jnp.minimum(jnp.maximum(result, -most), most).astype(kind)


def setup_inputs(seed: int = 0) -> dict:
    key_list = jax.random.split(jax.random.key(seed), 8)
    members = bell_draw(key_list[0], (MEMBERS, LEV, NLAT, NLON), 0.125, 0.75, ((0, 4), (2, 64)), jnp.float32)
    lat_root = draw_lat_root(jax.random.fold_in(key_list[7], 71), 0)
    lon_root = draw_lon_root(jax.random.fold_in(key_list[7], 71), 0)
    innovation = bell_draw(key_list[3], (NLAT, OBS_ROW), 1.0, 6.0, ((0, 64), (1, 4)), jnp.float32)
    obs_weight = jnp.clip(jnp.exp(math.log(4.0) - 2.0794415 * jax.random.uniform(key_list[4], (NLAT, OBS_ROW), jnp.float32) ** level_of(key_list[4], (NLAT, OBS_ROW), ((0, 64), (1, 4)), -0.2, 0.2)), 0.5, 4.0)
    obs_mask = plant((jax.random.randint(key_list[5], (NLAT, OBS_ROW), 0, 4) < 3).astype(jnp.int32), jax.random.fold_in(key_list[5], 1), 0, 1)
    obs_cell = draw_obs_cell(jax.random.fold_in(key_list[7], 71), 0)
    return dict(members=members, lat_root=lat_root, lon_root=lon_root, innovation=innovation, obs_weight=obs_weight, obs_mask=obs_mask, obs_cell=obs_cell)


HIGH = lax.Precision.HIGHEST


def root(field, lat_root, lon_root):
    inner = jnp.einsum("ij,mljn->mlin", lat_root, field, precision=HIGH)
    return jnp.einsum("mlin,kn->mlik", inner, lon_root, precision=HIGH)


def root_t(field, lat_root, lon_root):
    inner = jnp.einsum("ji,mljn->mlin", lat_root, field, precision=HIGH)
    return jnp.einsum("mlin,nk->mlik", inner, lon_root, precision=HIGH)


def reference(members, lat_root, lon_root, innovation, obs_weight, obs_mask, obs_cell):
    weights = obs_weight * obs_mask.astype(jnp.float32)
    row_ids = jnp.broadcast_to(jnp.arange(NLAT, dtype=jnp.int32)[:, None], obs_cell.shape)

    def forward(control):
        return jnp.sum(members * root(control, lat_root, lon_root), axis=0)

    def observe(field):
        flat = field.transpose(1, 0, 2).reshape(NLAT, LEV * NLON)
        return jnp.take_along_axis(flat, obs_cell, axis=1)

    def spread(values):
        flat = jnp.zeros((NLAT, LEV * NLON), jnp.float32).at[row_ids, obs_cell].add(values)
        field = flat.reshape(NLAT, LEV, NLON).transpose(1, 0, 2)
        return root_t(members * field[None], lat_root, lon_root)

    gradient = spread(-(weights * innovation))
    control = jnp.zeros_like(gradient)
    increment = jnp.zeros((LEV, NLAT, NLON), jnp.float32)
    norm_now = jnp.sum(gradient * gradient)
    for step in range(INNER):
        image = forward(gradient)
        curved = gradient + spread(weights * observe(image))
        length = norm_now / jnp.sum(gradient * curved)
        control = control - length * gradient
        increment = increment - length * image
        gradient = gradient - length * curved
        norm_now = jnp.sum(gradient * gradient)
    return increment, control
```

```python
import jax
import jax.numpy as jnp
from jax import lax
from jax.sharding import Mesh
from jax.sharding import PartitionSpec as P

LAT = ("lat_0", "lat_1", "lat_2", "lat_3")
MEM_LAT = ("mem", "lat_0", "lat_1", "lat_2", "lat_3")
HIGH = lax.Precision.HIGH


def per_device(members, lat_root, lon_root, innovation, obs_weight, obs_mask, obs_cell):
    mem_dev, levels, rows, nlon = members.shape
    fields = mem_dev * levels
    parts = lax.axis_size("mem")
    quarter = nlon // parts
    nlat = lat_root.shape[0]
    strips = nlat // rows
    per_field = strips // fields
    width = nlon // per_field
    weights = obs_weight * obs_mask.astype(jnp.float32)
    local_cell = obs_cell // nlon * quarter + obs_cell % quarter
    hit = local_cell[:, :, None] == jnp.arange(levels * quarter, dtype=jnp.int32)

    def on_grid(values):
        flat = jnp.sum(jnp.where(hit, values[:, :, None], 0.0), axis=1)
        return flat.reshape(rows, levels, quarter).transpose(1, 0, 2)

    def whole_rows(field):
        return lax.all_gather(field, "mem", axis=2, tiled=True)

    def to_strips(field):
        blocks = field.reshape(fields, rows, per_field, width).transpose(0, 2, 1, 3)
        blocks = blocks.reshape(strips, rows, width)
        out = lax.all_to_all(blocks, LAT, split_axis=0, concat_axis=0, tiled=True)
        return out.reshape(nlat, width)

    def to_rows(strip):
        out = lax.all_to_all(strip.reshape(strips, rows, width), LAT, split_axis=0, concat_axis=0, tiled=True)
        return out.reshape(fields, per_field, rows, width).transpose(0, 2, 1, 3).reshape(fields * rows, nlon)

    def gradient_of(field):
        member_field = (members * whole_rows(field)[None]).reshape(fields * rows, nlon)
        return jnp.dot(lat_root.T, to_strips(jnp.dot(member_field, lon_root, precision=HIGH)), precision=HIGH)

    def image_of(gradient):
        mixed = to_rows(jnp.dot(lat_root, gradient, precision=HIGH))
        value = jnp.dot(mixed, lon_root.T, precision=HIGH).reshape(members.shape)
        return lax.psum_scatter(jnp.sum(members * value, axis=0), "mem", scatter_dimension=2, tiled=True)

    weight_field = on_grid(weights)
    gradient0 = gradient_of(on_grid(-(weights * innovation)))
    image0 = image_of(gradient0)
    seen0 = weight_field * image0
    sums0 = lax.psum(jnp.stack([jnp.sum(gradient0 * gradient0), jnp.sum(seen0 * image0)]), MEM_LAT)
    gradient_z = gradient_of(seen0)
    image_z = image_of(gradient_z)
    length0 = sums0[0] / (sums0[0] + sums0[1])
    keep = 1.0 - length0
    gradient1 = keep * gradient0 - length0 * gradient_z
    image1 = keep * image0 - length0 * image_z
    sums1 = lax.psum(
        jnp.stack([jnp.sum(gradient1 * gradient1), jnp.sum(weight_field * image1 * image1)]), MEM_LAT
    )
    length1 = sums1[0] / (sums1[0] + sums1[1])
    control = to_rows(-(length0 * gradient0) - length1 * gradient1)
    increment = -(length0 * image0) - length1 * image1
    return increment, control.reshape(members.shape)


def solution(mesh):
    finer = Mesh(
        mesh.devices.reshape(mesh.shape["mem"], 4, 2, 4, 2),
        ("mem", "lat_0", "lat_1", "lat_2", "lat_3"),
    )
    placed = (P("mem", None, LAT, None), P(), P(), P(LAT, "mem"), P(LAT, "mem"), P(LAT, "mem"), P(LAT, "mem"))
    return jax.shard_map(
        per_device,
        mesh=finer,
        in_specs=placed,
        out_specs=(P(None, LAT, "mem"), P("mem", None, LAT, None)),
        check_vma=False,
    )
```

```python
import functools

import jax
import jax.numpy as jnp
from jax import lax
from jax.experimental import pallas as pl
from jax.experimental.pallas import tpu as pltpu
from jax.sharding import PartitionSpec as P

MESH = pl.DeviceIdType.MESH
F32 = jnp.float32
BF16 = jnp.bfloat16
NN = (((1,), (0,)), ((), ()))
NT = (((1,), (1,)), ((), ()))


def halves(x):
    high = x.astype(BF16)
    return high, (x - high.astype(F32)).astype(BF16)


def product(a, b, dims=NN):
    dot = functools.partial(lax.dot_general, dimension_numbers=dims, preferred_element_type=F32)
    return dot(a[0], b[0]) + (dot(a[0], b[1]) + dot(a[1], b[0]))


def kernel(
    members, a_hbm, b_hbm, innovation, obs_weight, obs_mask, obs_cell,
    increment, control,
    a_all, b_all, a_hi, a_lo, at_hi, at_lo, b_hi, b_lo, s_hi, s_lo,
    field, wfield, t_out, strip, grad, mixed, mixed_rows, grad_rows, value,
    part, got, image, sums, box_mem, box_a, box_b,
    load_sem, field_send, field_recv, t_send, t_recv, x_send, x_recv, g_send, g_recv,
    part_send, part_recv, mem_send, mem_recv, a_send, a_recv, b_send, b_recv,
):
    mem_dev, levels, rows, nlon = members.shape
    fields = mem_dev * levels
    parts = lax.axis_size("mem")
    strips = lax.axis_size("lat")
    per_field = strips // fields
    width = nlon // per_field
    nlat = strips * rows
    side = 8
    mem = lax.axis_index("mem")
    me = lax.axis_index("lat")
    my_field, my_part = me // per_field, me % per_field

    load_b = pltpu.make_async_copy(b_hbm, b_all, load_sem.at[0])
    load_a = pltpu.make_async_copy(a_hbm, a_all, load_sem.at[1])
    load_b.start()
    load_a.start()

    barrier = pltpu.get_barrier_semaphore()

    @pl.loop(1, strips)
    def _(k):
        pl.semaphore_signal(barrier, inc=1, device_id=(mem, (me + k) % strips), device_id_type=MESH)

    for k in range(1, parts):
        pl.semaphore_signal(barrier, inc=1, device_id=((mem + k) % parts, me), device_id_type=MESH)

    weights = obs_weight[...] * obs_mask[...].astype(F32)
    pulled = -(weights * innovation[...])
    cells = obs_cell[...]
    local = (cells // nlon) * width + cells % width
    spots = lax.broadcasted_iota(jnp.int32, (rows, levels * width), 1)
    wsum = jnp.zeros((rows, levels * width), F32)
    hsum = jnp.zeros((rows, levels * width), F32)
    for j in range(cells.shape[1]):
        hit = local[:, j : j + 1] == spots
        wsum = wsum + jnp.where(hit, weights[:, j : j + 1], 0.0)
        hsum = hsum + jnp.where(hit, pulled[:, j : j + 1], 0.0)
    for l in range(levels):
        wfield[l] = wsum[:, l * width : (l + 1) * width]
        field[0, mem, l] = hsum[:, l * width : (l + 1) * width]

    pl.semaphore_wait(barrier, strips - 1 + parts - 1)

    def bytes_of(ref, sem):
        return pltpu.make_async_copy(ref, ref, sem)

    def share_field(b):
        for k in range(1, parts):
            pltpu.make_async_remote_copy(
                src_ref=field.at[b, mem],
                dst_ref=field.at[b, mem],
                send_sem=field_send.at[b],
                recv_sem=field_recv.at[b],
                device_id=((mem + k) % parts, me),
                device_id_type=MESH,
            ).start()

    share_field(0)
    load_b.wait()
    for q in range(per_field):
        high, low = halves(b_all[:, q * width : (q + 1) * width])
        b_hi[q] = high
        b_lo[q] = low
    load_a.wait()
    high, low = halves(a_all[...])
    a_hi[...] = high
    a_lo[...] = low
    high, low = halves(a_all[...].T)
    at_hi[...] = high
    at_lo[...] = low

    def gradient_of(b):
        bytes_of(field.at[b, pl.ds(0, parts - 1)], field_recv.at[b]).wait()
        for q in range(per_field):
            high, low = halves(
                (members[:, :, :, q * width : (q + 1) * width] * field[b, q][None]).reshape(fields * rows, width)
            )
            s_hi[:, q * width : (q + 1) * width] = high
            s_lo[:, q * width : (q + 1) * width] = low

        @pl.loop(0, per_field)
        def _(t):
            q = (my_part + t) % per_field
            t_out[b, q] = product((s_hi[...], s_lo[...]), (b_hi[q], b_lo[q]))

            @pl.loop(0, fields)
            def _(k):
                f = (my_field + k) % fields
                d = f * per_field + q

                @pl.when(d != me)
                def _():
                    pltpu.make_async_remote_copy(
                        src_ref=t_out.at[b, q, pl.ds(f * rows, rows)],
                        dst_ref=strip.at[b, pl.ds(me * rows, rows)],
                        send_sem=t_send.at[b],
                        recv_sem=t_recv.at[b],
                        device_id=(mem, d),
                        device_id_type=MESH,
                    ).start()

                @pl.when(d == me)
                def _():
                    pltpu.make_async_copy(
                        t_out.at[b, q, pl.ds(f * rows, rows)], strip.at[b, pl.ds(me * rows, rows)], t_recv.at[b]
                    ).start()

        bytes_of(strip.at[b], t_recv.at[b]).wait()
        grad[b] = product((at_hi[...], at_lo[...]), halves(strip[b]))

    def to_rows(b, source, target, send, recv):
        @pl.loop(1, strips)
        def _(k):
            d = (me + k) % strips
            pltpu.make_async_remote_copy(
                src_ref=source.at[b, pl.ds(d * rows, rows)],
                dst_ref=target.at[b, my_part, pl.ds(my_field * rows, rows)],
                send_sem=send.at[b],
                recv_sem=recv.at[b, my_part],
                device_id=(mem, d),
                device_id_type=MESH,
            ).start()

        pltpu.make_async_copy(
            source.at[b, pl.ds(me * rows, rows)],
            target.at[b, my_part, pl.ds(my_field * rows, rows)],
            recv.at[b, my_part],
        ).start()

    def image_of(b):
        mixed[b] = product((a_hi[...], a_lo[...]), halves(grad[b]))
        to_rows(b, mixed, mixed_rows, x_send, x_recv)
        to_rows(b, grad, grad_rows, g_send, g_recv)
        for q in range(per_field):
            bytes_of(mixed_rows.at[b, q], x_recv.at[b, q]).wait()
            term = product(halves(mixed_rows[b, q]), (b_hi[q], b_lo[q]), NT)
            value[...] = term if q == 0 else value[...] + term
        for q in range(parts):
            shaped = value[:, q * width : (q + 1) * width].reshape(mem_dev, levels, rows, width)
            part[b, q] = jnp.sum(members[:, :, :, q * width : (q + 1) * width] * shaped, axis=0)
        for k in range(1, parts):
            other = (mem + k) % parts
            pltpu.make_async_remote_copy(
                src_ref=part.at[b, other],
                dst_ref=got.at[b, mem],
                send_sem=part_send.at[b],
                recv_sem=part_recv.at[b],
                device_id=(other, me),
                device_id_type=MESH,
            ).start()
        got[b, mem] = part[b, mem]
        bytes_of(got.at[b, pl.ds(0, parts - 1)], part_recv.at[b]).wait()
        image[b] = jnp.sum(got[b], axis=0)

    def lanes(x):
        return jnp.sum(x.reshape(-1, 8, 128), axis=0).sum(axis=0, keepdims=True)

    def start_round(b, box, slot, device, count, send, recv):
        @pl.loop(1, count)
        def _(k):
            pltpu.make_async_remote_copy(
                src_ref=sums.at[b],
                dst_ref=box.at[b, slot],
                send_sem=send.at[b],
                recv_sem=recv.at[b],
                device_id=device((slot + k) % count),
                device_id_type=MESH,
            ).start()

        box[b, slot] = sums[b]

    def end_round(b, box, count, send, recv):
        bytes_of(box.at[b, pl.ds(0, count - 1)], recv.at[b]).wait()
        bytes_of(box.at[b, pl.ds(0, count - 1)], send.at[b]).wait()
        sums[b] = jnp.sum(box[b], axis=0)

    def all_sums(b, norm, seen):
        row = lax.broadcasted_iota(jnp.int32, (8, 128), 0)
        sums[b] = jnp.where(row == 0, lanes(norm), 0.0) + jnp.where(row == 1, lanes(seen), 0.0)
        hi, lo = me // side, me % side
        start_round(b, box_mem, mem, lambda k: (k, me), parts, mem_send, mem_recv)
        end_round(b, box_mem, parts, mem_send, mem_recv)
        start_round(b, box_a, hi, lambda k: (mem, k * side + lo), side, a_send, a_recv)
        end_round(b, box_a, side, a_send, a_recv)
        start_round(b, box_b, lo, lambda k: (mem, hi * side + k), side, b_send, b_recv)
        end_round(b, box_b, side, b_send, b_recv)
        total = sums[b]
        norm = jnp.sum(total[0:1])
        return norm / (norm + jnp.sum(total[1:2]))

    def squares(x, w=None):
        y = x * x if w is None else x * x * w
        return (y[:, :128] + y[:, 128:]).reshape(-1, 8, 128)

    gradient_of(0)
    image_of(0)
    image0 = image[0]
    for l in range(levels):
        field[1, mem, l] = wfield[l] * image0[l]
    share_field(1)
    seen = squares(image0.reshape(levels * rows, width), wfield[...].reshape(levels * rows, width))
    norm0 = squares(grad[0])
    length0 = all_sums(0, norm0, seen)
    gradient_of(1)
    image_of(1)
    keep = 1.0 - length0
    image1 = keep * image0 - length0 * image[1]
    seen = squares(image1.reshape(levels * rows, width), wfield[...].reshape(levels * rows, width))
    norm1 = squares(keep * grad[0] - length0 * grad[1])
    length1 = all_sums(1, norm1, seen)
    first = -(length0 + length1 * keep)
    second = length1 * length0
    increment[...] = first * image0 + second * image[1]
    for b in range(2):
        for q in range(per_field):
            bytes_of(grad_rows.at[b, q], g_recv.at[b, q]).wait()
    for q in range(per_field):
        block = first * grad_rows[0, q] + second * grad_rows[1, q]
        control[:, :, :, q * width : (q + 1) * width] = block.reshape(mem_dev, levels, rows, width)
    for b in range(2):
        sent = strip.at[b, pl.ds(0, nlat - rows)]
        bytes_of(sent, t_send.at[b]).wait()
        bytes_of(sent, x_send.at[b]).wait()
        bytes_of(sent, g_send.at[b]).wait()
        bytes_of(field.at[b, pl.ds(0, parts - 1)], field_send.at[b]).wait()
        bytes_of(field.at[b, pl.ds(0, parts - 1)], part_send.at[b]).wait()


def solution(mesh):
    parts, strips = mesh.shape["mem"], mesh.shape["lat"]

    def per_device(members, lat_root, lon_root, innovation, obs_weight, obs_mask, obs_cell):
        mem_dev, levels, rows, nlon = members.shape
        nlat = lat_root.shape[0]
        fields = mem_dev * levels
        per_field = strips // fields
        width = nlon // per_field
        lines = fields * rows
        vmem = pl.BlockSpec(memory_space=pltpu.VMEM)
        whole = pl.BlockSpec(memory_space=pl.ANY)
        pair = pltpu.SemaphoreType.DMA((2,))
        quads = pltpu.SemaphoreType.DMA((2, per_field))
        scratch = [
            pltpu.VMEM((nlat, nlat), F32),
            pltpu.VMEM((nlon, nlon), F32),
            *[pltpu.VMEM((nlat, nlat), BF16)] * 4,
            *[pltpu.VMEM((per_field, nlon, width), BF16)] * 2,
            *[pltpu.VMEM((lines, nlon), BF16)] * 2,
            pltpu.VMEM((2, parts, levels, rows, width), F32),
            pltpu.VMEM((levels, rows, width), F32),
            pltpu.VMEM((2, per_field, lines, width), F32),
            *[pltpu.VMEM((2, nlat, width), F32)] * 3,
            *[pltpu.VMEM((2, per_field, lines, width), F32)] * 2,
            pltpu.VMEM((lines, nlon), F32),
            *[pltpu.VMEM((2, parts, levels, rows, width), F32)] * 2,
            pltpu.VMEM((2, levels, rows, width), F32),
            pltpu.VMEM((2, 8, 128), F32),
            pltpu.VMEM((2, parts, 8, 128), F32),
            pltpu.VMEM((2, 8, 8, 128), F32),
            pltpu.VMEM((2, 8, 8, 128), F32),
            pair,
            pair, pair, pair, pair,
            pair, quads, pair, quads,
            *[pair] * 8,
        ]
        return pl.pallas_call(
            kernel,
            out_shape=(
                jax.ShapeDtypeStruct((levels, rows, nlon // parts), F32),
                jax.ShapeDtypeStruct(members.shape, F32),
            ),
            in_specs=[vmem, whole, whole, vmem, vmem, vmem, vmem],
            out_specs=(vmem, vmem),
            scratch_shapes=scratch,
            compiler_params=pltpu.CompilerParams(
                collective_id=0, has_side_effects=True, vmem_limit_bytes=48 * 1024 * 1024
            ),
            cost_estimate=pl.CostEstimate(flops=5_000_000_000, bytes_accessed=7_000_000, transcendentals=0),
        )(members, lat_root, lon_root, innovation, obs_weight, obs_mask, obs_cell)

    return jax.shard_map(
        per_device,
        mesh=mesh,
        in_specs=(P("mem", None, "lat", None), P(), P(), *[P("lat", "mem")] * 4),
        out_specs=(P(None, "lat", "mem"), P("mem", None, "lat", None)),
        check_vma=False,
    )
```

```python
import functools

import jax
import jax.numpy as jnp
from jax import lax
from jax.experimental import pallas as pl
from jax.experimental.pallas import tpu as pltpu
from jax.sharding import PartitionSpec as P

MESH = pl.DeviceIdType.MESH
F32 = jnp.float32
BF16 = jnp.bfloat16
NN = (((1,), (0,)), ((), ()))
NT = (((1,), (1,)), ((), ()))


def halves(x):
    high = x.astype(BF16)
    return high, (x - high.astype(F32)).astype(BF16)


def product(a, b):
    dot = functools.partial(jnp.dot, preferred_element_type=F32)
    return dot(a[0], b[0]) + (dot(a[0], b[1]) + dot(a[1], b[0]))


def stacked_product(stack, b, dims):
    dot = functools.partial(lax.dot_general, dimension_numbers=dims, preferred_element_type=F32)
    lines = stack.shape[0] // 2
    both = dot(stack, b[0])
    return both[:lines] + (both[lines:] + dot(stack[:lines], b[1]))


def kernel(
    members_hbm, a_hbm, b_hbm, innovation_hbm, weight_hbm, mask_hbm, cell_hbm,
    increment, control,
    members, innovation, obs_weight, obs_mask, obs_cell, a_all, b_all, k_hi, k_lo, at_hi, at_lo, b_hi, b_lo, stack,
    field, wfield, t_out, strip, strip_hi, strip_lo, grad, mixed, mixed_rows, grad_rows, value,
    part, got, image, sums, box,
    load_sem, field_send, field_recv, t_send, t_recv, x_send, x_recv, g_send, g_recv,
    part_send, part_recv, box_send, box_recv,
):
    mem_dev, levels, rows, nlon = members.shape
    parts = lax.axis_size("mem")
    strips = lax.axis_size("lat")
    per_field = strips // (mem_dev * levels)
    width = nlon // per_field
    nlat = strips * rows
    lines = mem_dev * rows
    mem = lax.axis_index("mem")
    me = lax.axis_index("lat")

    side = 4
    x, z, y, core = me // 16, me // 8 % 2, me // 2 % 4, me % 2
    column = mem * side + z * 2 + core
    plane = x * side + y
    my_member, my_part = x * 2 + z, (x + y) % per_field

    def strip_device(m, l, q):
        return m // 2 * 16 + m % 2 * 8 + (q - m // 2 + per_field) % per_field * 2 + l

    def in_column(k):
        return k // side, x * 16 + k % side // 2 * 8 + y * 2 + k % 2

    def in_plane(k):
        return mem, k // side * 16 + z * 8 + k % side * 2 + core

    loads = [
        pltpu.make_async_copy(source, target, load_sem.at[k])
        for k, (source, target) in enumerate([
            (weight_hbm, obs_weight), (mask_hbm, obs_mask), (innovation_hbm, innovation), (cell_hbm, obs_cell),
            (b_hbm, b_all), (members_hbm, members), (a_hbm, a_all),
        ])
    ]
    for load in loads:
        load.start()

    barrier = pltpu.get_barrier_semaphore()

    @pl.loop(1, strips)
    def _(k):
        pl.semaphore_signal(barrier, inc=1, device_id=(mem, (me + k) % strips), device_id_type=MESH)

    @pl.loop(0, parts * side)
    def _(k):
        @pl.when(k // side != mem)
        def _():
            pl.semaphore_signal(barrier, inc=1, device_id=in_column(k), device_id_type=MESH)

    for load in loads[:4]:
        load.wait()
    weights = obs_weight[...] * obs_mask[...].astype(F32)
    pulled = -(weights * innovation[...])
    cells = obs_cell[...]
    local = (cells // nlon) * width + cells % width
    spots = lax.broadcasted_iota(jnp.int32, (rows, levels * width), 1)
    wsum = jnp.zeros((rows, levels * width), F32)
    hsum = jnp.zeros((rows, levels * width), F32)
    for j in range(cells.shape[1]):
        hit = local[:, j : j + 1] == spots
        wsum = wsum + jnp.where(hit, weights[:, j : j + 1], 0.0)
        hsum = hsum + jnp.where(hit, pulled[:, j : j + 1], 0.0)
    for l in range(levels):
        wfield[l] = wsum[:, l * width : (l + 1) * width]
        field[0, l, mem] = hsum[:, l * width : (l + 1) * width]

    pl.semaphore_wait(barrier, strips - 1 + (parts - 1) * side)

    def bytes_of(ref, sem):
        return pltpu.make_async_copy(ref, ref, sem)

    def share_field(b, l):
        for k in range(1, parts):
            pltpu.make_async_remote_copy(
                src_ref=field.at[b, l, mem],
                dst_ref=field.at[b, l, mem],
                send_sem=field_send.at[b, l],
                recv_sem=field_recv.at[b, l],
                device_id=((mem + k) % parts, me),
                device_id_type=MESH,
            ).start()

    for l in range(levels):
        share_field(0, l)
    loads[4].wait()
    for q in range(per_field):
        high, low = halves(b_all[:, q * width : (q + 1) * width])
        b_hi[q] = high
        b_lo[q] = low
    loads[6].wait()
    transposed = halves(a_all[...].T)
    at_hi[...], at_lo[...] = transposed
    k_hi[...], k_lo[...] = halves(product(halves(a_all[...]), transposed))
    loads[5].wait()

    def sent_strips(b, l):
        @pl.when(core == l)
        def _():
            bytes_of(strip.at[b, pl.ds(0, (strips // levels - 1) * rows)], t_send.at[b, l]).wait()

        @pl.when(core != l)
        def _():
            bytes_of(strip.at[b, pl.ds(0, strips // levels * rows)], t_send.at[b, l]).wait()

    def strips_of(b, l):
        bytes_of(field.at[b, l, pl.ds(0, parts - 1)], field_recv.at[b, l]).wait()
        for q in range(per_field):
            block = (members[:, l, :, q * width : (q + 1) * width] * field[b, l, q][None]).reshape(lines, width)
            high, low = halves(block)
            stack[:lines, q * width : (q + 1) * width] = high
            stack[lines:, q * width : (q + 1) * width] = low

        @pl.loop(0, per_field)
        def _(t):
            q = (my_part + t) % per_field
            t_out[b, l, q] = stacked_product(stack[...], (b_hi[q], b_lo[q]), NN)
            if l:

                @pl.when(t == 0)
                def _():
                    sent_strips(b, 0)

            @pl.loop(0, mem_dev)
            def _(k):
                m = (x + 6 - k // 2) % 4 * 2 + (z + k + 1) % 2
                d = strip_device(m, l, q)

                @pl.when(d != me)
                def _():
                    pltpu.make_async_remote_copy(
                        src_ref=t_out.at[b, l, q, pl.ds(m * rows, rows)],
                        dst_ref=strip.at[b, pl.ds(me * rows, rows)],
                        send_sem=t_send.at[b, l],
                        recv_sem=t_recv.at[b],
                        device_id=(mem, d),
                        device_id_type=MESH,
                    ).start()

                @pl.when(d == me)
                def _():
                    pltpu.make_async_copy(
                        t_out.at[b, l, q, pl.ds(m * rows, rows)], strip.at[b, pl.ds(me * rows, rows)], t_recv.at[b]
                    ).start()

    def to_rows(b, source, target, send, recv, pieces):
        mine = target.at[b, core, my_part, pl.ds(my_member * rows, rows)]
        for dx, piece in zip((2, 1, 3, 0), pieces):

            def send_one(k, dx=dx):
                d = (x + dx) % 4 * 16 + (z + k // 2 + 1) % 2 * 8 + (y + 6 - k // 4) % 4 * 2 + (core + k + 1) % 2
                pltpu.make_async_remote_copy(
                    src_ref=source.at[b, pl.ds(d * rows, rows)],
                    dst_ref=mine,
                    send_sem=send.at[b],
                    recv_sem=recv.at[b, core, my_part],
                    device_id=(mem, d),
                    device_id_type=MESH,
                ).start()

            if piece is not None:
                at = pl.ds((x + dx) % 4 * 16 * rows, 16 * rows)
                source[b, at] = piece(at)
            if dx:

                @pl.loop(0, 16)
                def _(k):
                    send_one(k)
            else:

                @pl.loop(0, 16)
                def _(k):
                    @pl.when(k != 11)
                    def _():
                        send_one(k)

        pltpu.make_async_copy(source.at[b, pl.ds(me * rows, rows)], mine, recv.at[b, core, my_part]).start()

    def mix(b):
        bytes_of(strip.at[b], t_recv.at[b]).wait()
        high, low = halves(strip[b])
        strip_hi[b] = high
        strip_lo[b] = low
        to_rows(
            b, mixed, mixed_rows, x_send, x_recv,
            [lambda at: product((k_hi[at], k_lo[at]), (high, low))] * 4,
        )

    def gradient_of(b):
        grad[b] = product((at_hi[...], at_lo[...]), (strip_hi[b], strip_lo[b]))

    def send_gradient(b):
        to_rows(b, grad, grad_rows, g_send, g_recv, [None] * 4)

    def part_of(b, l):
        for q in range(per_field):
            bytes_of(mixed_rows.at[b, l, q], x_recv.at[b, l, q]).wait()
            term = stacked_product(jnp.concatenate(halves(mixed_rows[b, l, q]), axis=0), (b_hi[q], b_lo[q]), NT)
            value[...] = term if q == 0 else value[...] + term
        for q in range(parts):
            shaped = value[:, q * width : (q + 1) * width].reshape(mem_dev, rows, width)
            part[b, l, q] = jnp.sum(members[:, l, :, q * width : (q + 1) * width] * shaped, axis=0)
        for k in range(1, parts):
            other = (mem + k) % parts
            pltpu.make_async_remote_copy(
                src_ref=part.at[b, l, other],
                dst_ref=got.at[b, l, mem],
                send_sem=part_send.at[b, l],
                recv_sem=part_recv.at[b, l],
                device_id=(other, me),
                device_id_type=MESH,
            ).start()
        got[b, l, mem] = part[b, l, mem]

    def image_of(b, l):
        bytes_of(got.at[b, l, pl.ds(0, parts - 1)], part_recv.at[b, l]).wait()
        image[b, l] = jnp.sum(got[b, l], axis=0)

    def lanes(x):
        return jnp.sum(x.reshape(-1, 8, 128), axis=0).sum(axis=0, keepdims=True)

    def start_round(b, n, slot, device):
        @pl.loop(1, parts * side)
        def _(k):
            pltpu.make_async_remote_copy(
                src_ref=sums.at[b, n],
                dst_ref=box.at[b, n, slot],
                send_sem=box_send.at[b, n],
                recv_sem=box_recv.at[b, n],
                device_id=device((slot + k) % (parts * side)),
                device_id_type=MESH,
            ).start()

        box[b, n, slot] = sums[b, n]

    def end_round(b, n):
        bytes_of(box.at[b, n, pl.ds(0, parts * side - 1)], box_recv.at[b, n]).wait()
        return jnp.sum(box[b, n], axis=0)

    def start_sums(b, norm, seen):
        row = lax.broadcasted_iota(jnp.int32, (8, 128), 0)
        sums[b, 0] = jnp.where(row == 0, lanes(norm), 0.0) + jnp.where(row == 1, lanes(seen), 0.0)
        start_round(b, 0, column, in_column)

    def pass_sums(b):
        sums[b, 1] = end_round(b, 0)
        start_round(b, 1, plane, in_plane)

    def end_sums(b):
        total = end_round(b, 1)
        norm = jnp.sum(total[0:1])
        return norm / (norm + jnp.sum(total[1:2]))

    def squares(x, w=None):
        y = x * x if w is None else x * x * w
        return (y[:, :128] + y[:, 128:]).reshape(-1, 8, 128)

    flat_weights = wfield[...].reshape(levels * rows, width)
    for l in range(levels):
        strips_of(0, l)
    mix(0)
    gradient_of(0)
    norm = squares(grad[0])
    for l in range(levels):
        part_of(0, l)
    for l in range(levels):
        image_of(0, l)
        field[1, l, mem] = wfield[l] * image[0, l]
        share_field(1, l)
    image0 = image[0]
    start_sums(0, norm, squares(image0.reshape(levels * rows, width), flat_weights))
    for l in range(levels):
        strips_of(1, l)
    mix(1)
    pass_sums(0)
    gradient_of(1)
    send_gradient(0)
    for l in range(levels):
        part_of(1, l)
    send_gradient(1)
    length0 = end_sums(0)
    keep = 1.0 - length0
    norm = squares(keep * grad[0] - length0 * grad[1])
    for l in range(levels):
        image_of(1, l)
    image1 = keep * image0 - length0 * image[1]
    start_sums(1, norm, squares(image1.reshape(levels * rows, width), flat_weights))
    pass_sums(1)
    length1 = end_sums(1)
    first = -(length0 + length1 * keep)
    second = length1 * length0
    increment[...] = first * image0 + second * image[1]
    for l in range(levels):
        for q in range(per_field):
            for b in range(2):
                bytes_of(grad_rows.at[b, l, q], g_recv.at[b, l, q]).wait()
            block = first * grad_rows[0, l, q] + second * grad_rows[1, l, q]
            control[:, l, :, q * width : (q + 1) * width] = block.reshape(mem_dev, rows, width)
    for b in range(2):
        sent = strip.at[b, pl.ds(0, nlat - rows)]
        bytes_of(sent, x_send.at[b]).wait()
        bytes_of(sent, g_send.at[b]).wait()
        sent_strips(b, 1)
        for l in range(levels):
            bytes_of(field.at[b, l, pl.ds(0, parts - 1)], field_send.at[b, l]).wait()
            bytes_of(field.at[b, l, pl.ds(0, parts - 1)], part_send.at[b, l]).wait()
        for n in range(2):
            bytes_of(box.at[b, n, pl.ds(0, parts * side - 1)], box_send.at[b, n]).wait()


def solution(mesh):
    parts, strips = mesh.shape["mem"], mesh.shape["lat"]

    def per_device(members, lat_root, lon_root, innovation, obs_weight, obs_mask, obs_cell):
        mem_dev, levels, rows, nlon = members.shape
        nlat = lat_root.shape[0]
        per_field = strips // (mem_dev * levels)
        width = nlon // per_field
        lines = mem_dev * rows
        vmem = pl.BlockSpec(memory_space=pltpu.VMEM)
        whole = pl.BlockSpec(memory_space=pltpu.HBM)
        slots = innovation.shape
        pair = pltpu.SemaphoreType.DMA((2,))
        levelled = pltpu.SemaphoreType.DMA((2, levels))
        quads = pltpu.SemaphoreType.DMA((2, levels, per_field))
        scratch = [
            pltpu.VMEM(members.shape, F32),
            *[pltpu.VMEM(slots, F32)] * 2,
            *[pltpu.VMEM(slots, jnp.int32)] * 2,
            pltpu.VMEM((nlat, nlat), F32),
            pltpu.VMEM((nlon, nlon), F32),
            *[pltpu.VMEM((nlat, nlat), BF16)] * 4,
            *[pltpu.VMEM((per_field, nlon, width), BF16)] * 2,
            pltpu.VMEM((2 * lines, nlon), BF16),
            pltpu.VMEM((2, levels, parts, rows, width), F32),
            pltpu.VMEM((levels, rows, width), F32),
            pltpu.VMEM((2, levels, per_field, lines, width), F32),
            pltpu.VMEM((2, nlat, width), F32),
            *[pltpu.VMEM((2, nlat, width), BF16)] * 2,
            *[pltpu.VMEM((2, nlat, width), F32)] * 2,
            *[pltpu.VMEM((2, levels, per_field, lines, width), F32)] * 2,
            pltpu.VMEM((lines, nlon), F32),
            *[pltpu.VMEM((2, levels, parts, rows, width), F32)] * 2,
            pltpu.VMEM((2, levels, rows, width), F32),
            pltpu.VMEM((2, 2, 8, 128), F32),
            pltpu.VMEM((2, 2, 16, 8, 128), F32),
            pltpu.SemaphoreType.DMA((7,)),
            levelled, levelled, levelled, pair,
            pair, quads, pair, quads,
            levelled, levelled,
            *[pltpu.SemaphoreType.DMA((2, 2))] * 2,
        ]
        return pl.pallas_call(
            kernel,
            out_shape=(
                jax.ShapeDtypeStruct((levels, rows, nlon // parts), F32),
                jax.ShapeDtypeStruct(members.shape, F32),
            ),
            in_specs=[whole] * 7,
            out_specs=(vmem, vmem),
            scratch_shapes=scratch,
            compiler_params=pltpu.CompilerParams(
                collective_id=0, has_side_effects=True, vmem_limit_bytes=62 * 1024 * 1024
            ),
            cost_estimate=pl.CostEstimate(flops=5_000_000_000, bytes_accessed=7_000_000, transcendentals=0),
        )(members, lat_root, lon_root, innovation, obs_weight, obs_mask, obs_cell)

    return jax.shard_map(
        per_device,
        mesh=mesh,
        in_specs=(P("mem", None, "lat", None), P(), P(), *[P("lat", "mem")] * 4),
        out_specs=(P(None, "lat", "mem"), P("mem", None, "lat", None)),
        check_vma=False,
    )
```

```python
import functools

import jax
import jax.numpy as jnp
from jax import lax
from jax.experimental import pallas as pl
from jax.experimental.pallas import tpu as pltpu
from jax.sharding import PartitionSpec as P

MESH = pl.DeviceIdType.MESH
F32 = jnp.float32
BF16 = jnp.bfloat16
NN = (((1,), (0,)), ((), ()))
NT = (((1,), (1,)), ((), ()))


def halves(x):
    high = x.astype(BF16)
    return high, (x - high.astype(F32)).astype(BF16)


def product(a, b):
    dot = functools.partial(jnp.dot, preferred_element_type=F32)
    return dot(a[0], b[0]) + (dot(a[0], b[1]) + dot(a[1], b[0]))


def stacked_product(stack, b, dims):
    dot = functools.partial(lax.dot_general, dimension_numbers=dims, preferred_element_type=F32)
    lines = stack.shape[0] // 2
    both = dot(stack, b[0])
    return both[:lines] + (both[lines:] + dot(stack[:lines], b[1]))


def kernel(
    members_hbm, a_hbm, b_hbm, innovation_hbm, weight_hbm, mask_hbm, cell_hbm,
    increment, control,
    members, innovation, obs_weight, obs_mask, obs_cell, a_all, b_all, k_hi, k_lo, at_hi, at_lo, b_hi, b_lo, stack,
    field, wfield, t_out, strip, strip_hi, strip_lo, grad, mixed, mixed_rows, grad_rows, value,
    part, got, all_parts, image, sums, box,
    load_sem, w_send, w_recv, field_send, field_recv, t_send, t_recv, x_send, x_recv, g_send, g_recv,
    part_send, part_recv, box_send, box_recv,
):
    mem_dev, levels, rows, nlon = members.shape
    parts = lax.axis_size("mem")
    strips = lax.axis_size("lat")
    per_field = strips // (mem_dev * levels)
    width = nlon // per_field
    nlat = strips * rows
    lines = mem_dev * rows
    mem = lax.axis_index("mem")
    me = lax.axis_index("lat")

    side = 4
    x, z, y, core = me // 16, me // 8 % 2, me // 2 % 4, me % 2
    column = mem * side + z * 2 + core
    plane = x * side + y
    my_member, my_part = x * 2 + z, (x + y) % per_field

    def strip_device(m, l, q):
        return m // 2 * 16 + m % 2 * 8 + (q - m // 2 + per_field) % per_field * 2 + l

    def in_column(k):
        return k // side, x * 16 + k % side // 2 * 8 + y * 2 + k % 2

    def in_plane(k):
        return mem, k // side * 16 + z * 8 + k % side * 2 + core

    loads = [
        pltpu.make_async_copy(source, target, load_sem.at[k])
        for k, (source, target) in enumerate([
            (weight_hbm, obs_weight), (mask_hbm, obs_mask), (innovation_hbm, innovation), (cell_hbm, obs_cell),
            (b_hbm, b_all), (members_hbm, members), (a_hbm, a_all),
        ])
    ]
    barrier = pltpu.get_barrier_semaphore()

    @pl.loop(1, strips)
    def _(k):
        pl.semaphore_signal(barrier, inc=1, device_id=(mem, (me + k) % strips), device_id_type=MESH)

    @pl.loop(0, parts * side)
    def _(k):
        @pl.when(k // side != mem)
        def _():
            pl.semaphore_signal(barrier, inc=1, device_id=in_column(k), device_id_type=MESH)

    for load in loads:
        load.start()
    for load in loads[:4]:
        load.wait()
    weights = obs_weight[...] * obs_mask[...].astype(F32)
    pulled = -(weights * innovation[...])
    cells = obs_cell[...]
    local = (cells // nlon) * width + cells % width
    spots = lax.broadcasted_iota(jnp.int32, (rows, levels * width), 1)
    wsum = jnp.zeros((rows, levels * width), F32)
    hsum = jnp.zeros((rows, levels * width), F32)
    for j in range(cells.shape[1]):
        hit = local[:, j : j + 1] == spots
        wsum = wsum + jnp.where(hit, weights[:, j : j + 1], 0.0)
        hsum = hsum + jnp.where(hit, pulled[:, j : j + 1], 0.0)
    for l in range(levels):
        wfield[l, mem] = wsum[:, l * width : (l + 1) * width]
        field[0, l, mem] = hsum[:, l * width : (l + 1) * width]

    pl.semaphore_wait(barrier, strips - 1 + (parts - 1) * side)

    def bytes_of(ref, sem):
        return pltpu.make_async_copy(ref, ref, sem)

    def to_column(source, target, send, recv):
        for k in range(1, parts):
            pltpu.make_async_remote_copy(
                src_ref=source,
                dst_ref=target,
                send_sem=send,
                recv_sem=recv,
                device_id=((mem + k) % parts, me),
                device_id_type=MESH,
            ).start()

    for l in range(levels):
        to_column(field.at[0, l, mem], field.at[0, l, mem], field_send.at[0, l], field_recv.at[0, l])
    to_column(wfield.at[:, mem], wfield.at[:, mem], w_send.at[0], w_recv.at[0])
    loads[4].wait()
    for q in range(per_field):
        high, low = halves(b_all[:, q * width : (q + 1) * width])
        b_hi[q] = high
        b_lo[q] = low
    loads[6].wait()
    transposed = halves(a_all[...].T)
    at_hi[...], at_lo[...] = transposed
    k_hi[...], k_lo[...] = halves(product(halves(a_all[...]), transposed))
    loads[5].wait()

    def sent_strips(b, l):
        @pl.when(core == l)
        def _():
            bytes_of(strip.at[b, pl.ds(0, (strips // levels - 1) * rows)], t_send.at[b, l]).wait()

        @pl.when(core != l)
        def _():
            bytes_of(strip.at[b, pl.ds(0, strips // levels * rows)], t_send.at[b, l]).wait()

    def strips_of(b, l):
        if b == 0:
            bytes_of(field.at[0, l, pl.ds(0, parts - 1)], field_recv.at[0, l]).wait()
        for q in range(per_field):
            block = (members[:, l, :, q * width : (q + 1) * width] * field[b, l, q][None]).reshape(lines, width)
            high, low = halves(block)
            stack[:lines, q * width : (q + 1) * width] = high
            stack[lines:, q * width : (q + 1) * width] = low

        @pl.loop(0, per_field)
        def _(t):
            q = (my_part + t) % per_field
            t_out[b, l, q] = stacked_product(stack[...], (b_hi[q], b_lo[q]), NN)
            if l:

                @pl.when(t == 0)
                def _():
                    sent_strips(b, 0)

            @pl.loop(0, mem_dev)
            def _(k):
                m = (x + 6 - k // 2) % 4 * 2 + (z + k + 1) % 2
                d = strip_device(m, l, q)

                @pl.when(d != me)
                def _():
                    pltpu.make_async_remote_copy(
                        src_ref=t_out.at[b, l, q, pl.ds(m * rows, rows)],
                        dst_ref=strip.at[b, pl.ds(me * rows, rows)],
                        send_sem=t_send.at[b, l],
                        recv_sem=t_recv.at[b],
                        device_id=(mem, d),
                        device_id_type=MESH,
                    ).start()

                @pl.when(d == me)
                def _():
                    pltpu.make_async_copy(
                        t_out.at[b, l, q, pl.ds(m * rows, rows)], strip.at[b, pl.ds(me * rows, rows)], t_recv.at[b]
                    ).start()

    def to_rows(b, source, target, send, recv, pieces):
        mine = target.at[b, core, my_part, pl.ds(my_member * rows, rows)]
        for dx, piece in zip((2, 1, 3, 0), pieces):

            def send_one(k, dx=dx):
                d = (x + dx) % 4 * 16 + (z + k // 2 + 1) % 2 * 8 + (y + 6 - k // 4) % 4 * 2 + (core + k + 1) % 2
                pltpu.make_async_remote_copy(
                    src_ref=source.at[b, pl.ds(d * rows, rows)],
                    dst_ref=mine,
                    send_sem=send.at[b],
                    recv_sem=recv.at[b, core, my_part],
                    device_id=(mem, d),
                    device_id_type=MESH,
                ).start()

            if piece is not None:
                at = pl.ds((x + dx) % 4 * 16 * rows, 16 * rows)
                source[b, at] = piece(at)
            if dx:

                @pl.loop(0, 16)
                def _(k):
                    send_one(k)
            else:

                @pl.loop(0, 16)
                def _(k):
                    @pl.when(k != 11)
                    def _():
                        send_one(k)

        pltpu.make_async_copy(source.at[b, pl.ds(me * rows, rows)], mine, recv.at[b, core, my_part]).start()

    def mix(b):
        bytes_of(strip.at[b], t_recv.at[b]).wait()
        high, low = halves(strip[b])
        strip_hi[b] = high
        strip_lo[b] = low
        to_rows(
            b, mixed, mixed_rows, x_send, x_recv,
            [lambda at: product((k_hi[at], k_lo[at]), (high, low))] * 4,
        )

    def gradient_of(b):
        grad[b] = product((at_hi[...], at_lo[...]), (strip_hi[b], strip_lo[b]))

    def send_gradient(b):
        to_rows(b, grad, grad_rows, g_send, g_recv, [None] * 4)

    def part_of(b, l):
        for q in range(per_field):
            bytes_of(mixed_rows.at[b, l, q], x_recv.at[b, l, q]).wait()
            term = stacked_product(jnp.concatenate(halves(mixed_rows[b, l, q]), axis=0), (b_hi[q], b_lo[q]), NT)
            value[...] = term if q == 0 else value[...] + term
        for q in range(parts):
            shaped = value[:, q * width : (q + 1) * width].reshape(mem_dev, rows, width)
            part[b, l, q] = jnp.sum(members[:, l, :, q * width : (q + 1) * width] * shaped, axis=0)
        if b == 0:
            to_column(part.at[0, l], all_parts.at[l, mem], part_send.at[0, l], part_recv.at[0, l])
            all_parts[l, mem] = part[0, l]
            return
        for k in range(1, parts):
            other = (mem + k) % parts
            pltpu.make_async_remote_copy(
                src_ref=part.at[b, l, other],
                dst_ref=got.at[b, l, mem],
                send_sem=part_send.at[b, l],
                recv_sem=part_recv.at[b, l],
                device_id=(other, me),
                device_id_type=MESH,
            ).start()
        got[b, l, mem] = part[b, l, mem]

    def image_of(b, l):
        if b == 0:
            bytes_of(all_parts.at[l, pl.ds(0, parts - 1)], part_recv.at[0, l]).wait()
            for q in range(parts):
                whole = jnp.sum(all_parts[l, :, q], axis=0)
                field[1, l, q] = wfield[l, q] * whole
            image[0, l] = jnp.sum(all_parts[l, :, mem], axis=0)
            return
        bytes_of(got.at[b, l, pl.ds(0, parts - 1)], part_recv.at[b, l]).wait()
        image[b, l] = jnp.sum(got[b, l], axis=0)

    def lanes(x):
        return jnp.sum(x.reshape(-1, 8, 128), axis=0).sum(axis=0, keepdims=True)

    def start_round(b, n, slot, device):
        @pl.loop(1, parts * side)
        def _(k):
            pltpu.make_async_remote_copy(
                src_ref=sums.at[b, n],
                dst_ref=box.at[b, n, slot],
                send_sem=box_send.at[b, n],
                recv_sem=box_recv.at[b, n],
                device_id=device((slot + k) % (parts * side)),
                device_id_type=MESH,
            ).start()

        box[b, n, slot] = sums[b, n]

    def end_round(b, n):
        bytes_of(box.at[b, n, pl.ds(0, parts * side - 1)], box_recv.at[b, n]).wait()
        return jnp.sum(box[b, n], axis=0)

    def start_sums(b, norm, seen):
        row = lax.broadcasted_iota(jnp.int32, (8, 128), 0)
        sums[b, 0] = jnp.where(row == 0, lanes(norm), 0.0) + jnp.where(row == 1, lanes(seen), 0.0)
        start_round(b, 0, column, in_column)

    def pass_sums(b):
        sums[b, 1] = end_round(b, 0)
        start_round(b, 1, plane, in_plane)

    def end_sums(b):
        total = end_round(b, 1)
        norm = jnp.sum(total[0:1])
        return norm / (norm + jnp.sum(total[1:2]))

    def squares(x, w=None):
        y = x * x if w is None else x * x * w
        return (y[:, :128] + y[:, 128:]).reshape(-1, 8, 128)

    for l in range(levels):
        strips_of(0, l)
    mix(0)
    gradient_of(0)
    norm = squares(grad[0])
    for l in range(levels):
        part_of(0, l)
    bytes_of(mixed.at[0, pl.ds(0, (parts - 1) * levels * rows)], w_recv.at[0]).wait()
    image_of(0, 0)
    strips_of(1, 0)
    image_of(0, 1)
    flat_weights = wfield[:, mem].reshape(levels * rows, width)
    image0 = image[0]
    start_sums(0, norm, squares(image0.reshape(levels * rows, width), flat_weights))
    strips_of(1, 1)
    mix(1)
    pass_sums(0)
    gradient_of(1)
    send_gradient(0)
    for l in range(levels):
        part_of(1, l)
    send_gradient(1)
    length0 = end_sums(0)
    keep = 1.0 - length0
    norm = squares(keep * grad[0] - length0 * grad[1])
    for l in range(levels):
        image_of(1, l)
    image1 = keep * image0 - length0 * image[1]
    start_sums(1, norm, squares(image1.reshape(levels * rows, width), flat_weights))
    pass_sums(1)
    length1 = end_sums(1)
    first = -(length0 + length1 * keep)
    second = length1 * length0
    increment[...] = first * image0 + second * image[1]
    for l in range(levels):
        for q in range(per_field):
            for b in range(2):
                bytes_of(grad_rows.at[b, l, q], g_recv.at[b, l, q]).wait()
            block = first * grad_rows[0, l, q] + second * grad_rows[1, l, q]
            control[:, l, :, q * width : (q + 1) * width] = block.reshape(mem_dev, rows, width)
    bytes_of(mixed.at[0, pl.ds(0, (parts - 1) * levels * rows)], w_send.at[0]).wait()
    for b in range(2):
        sent = strip.at[b, pl.ds(0, nlat - rows)]
        bytes_of(sent, x_send.at[b]).wait()
        bytes_of(sent, g_send.at[b]).wait()
        sent_strips(b, 1)
        for l in range(levels):
            if b == 0:
                bytes_of(field.at[0, l, pl.ds(0, parts - 1)], field_send.at[0, l]).wait()
                bytes_of(all_parts.at[l, pl.ds(0, parts - 1)], part_send.at[0, l]).wait()
            else:
                bytes_of(field.at[b, l, pl.ds(0, parts - 1)], part_send.at[b, l]).wait()
        for n in range(2):
            bytes_of(box.at[b, n, pl.ds(0, parts * side - 1)], box_send.at[b, n]).wait()


def solution(mesh):
    parts, strips = mesh.shape["mem"], mesh.shape["lat"]

    def per_device(members, lat_root, lon_root, innovation, obs_weight, obs_mask, obs_cell):
        mem_dev, levels, rows, nlon = members.shape
        nlat = lat_root.shape[0]
        per_field = strips // (mem_dev * levels)
        width = nlon // per_field
        lines = mem_dev * rows
        vmem = pl.BlockSpec(memory_space=pltpu.VMEM)
        whole = pl.BlockSpec(memory_space=pltpu.HBM)
        slots = innovation.shape
        pair = pltpu.SemaphoreType.DMA((2,))
        levelled = pltpu.SemaphoreType.DMA((2, levels))
        quads = pltpu.SemaphoreType.DMA((2, levels, per_field))
        scratch = [
            pltpu.VMEM(members.shape, F32),
            *[pltpu.VMEM(slots, F32)] * 2,
            *[pltpu.VMEM(slots, jnp.int32)] * 2,
            pltpu.VMEM((nlat, nlat), F32),
            pltpu.VMEM((nlon, nlon), F32),
            *[pltpu.VMEM((nlat, nlat), BF16)] * 4,
            *[pltpu.VMEM((per_field, nlon, width), BF16)] * 2,
            pltpu.VMEM((2 * lines, nlon), BF16),
            pltpu.VMEM((2, levels, parts, rows, width), F32),
            pltpu.VMEM((levels, parts, rows, width), F32),
            pltpu.VMEM((2, levels, per_field, lines, width), F32),
            pltpu.VMEM((2, nlat, width), F32),
            *[pltpu.VMEM((2, nlat, width), BF16)] * 2,
            *[pltpu.VMEM((2, nlat, width), F32)] * 2,
            *[pltpu.VMEM((2, levels, per_field, lines, width), F32)] * 2,
            pltpu.VMEM((lines, nlon), F32),
            *[pltpu.VMEM((2, levels, parts, rows, width), F32)] * 2,
            pltpu.VMEM((levels, parts, parts, rows, width), F32),
            pltpu.VMEM((2, levels, rows, width), F32),
            pltpu.VMEM((2, 2, 8, 128), F32),
            pltpu.VMEM((2, 2, 16, 8, 128), F32),
            pltpu.SemaphoreType.DMA((7,)),
            *[pltpu.SemaphoreType.DMA((1,))] * 2,
            levelled, levelled, levelled, pair,
            pair, quads, pair, quads,
            levelled, levelled,
            *[pltpu.SemaphoreType.DMA((2, 2))] * 2,
        ]
        return pl.pallas_call(
            kernel,
            out_shape=(
                jax.ShapeDtypeStruct((levels, rows, nlon // parts), F32),
                jax.ShapeDtypeStruct(members.shape, F32),
            ),
            in_specs=[whole] * 7,
            out_specs=(vmem, vmem),
            scratch_shapes=scratch,
            compiler_params=pltpu.CompilerParams(
                collective_id=0, has_side_effects=True, vmem_limit_bytes=62 * 1024 * 1024
            ),
            cost_estimate=pl.CostEstimate(flops=5_000_000_000, bytes_accessed=7_000_000, transcendentals=0),
        )(members, lat_root, lon_root, innovation, obs_weight, obs_mask, obs_cell)

    return jax.shard_map(
        per_device,
        mesh=mesh,
        in_specs=(P("mem", None, "lat", None), P(), P(), *[P("lat", "mem")] * 4),
        out_specs=(P(None, "lat", "mem"), P("mem", None, "lat", None)),
        check_vma=False,
    )
```

```python
import functools

import jax
import jax.numpy as jnp
from jax import lax
from jax.experimental import pallas as pl
from jax.experimental.pallas import tpu as pltpu
from jax.sharding import PartitionSpec as P

MESH = pl.DeviceIdType.MESH
F32 = jnp.float32
BF16 = jnp.bfloat16
NN = (((1,), (0,)), ((), ()))
NT = (((1,), (1,)), ((), ()))


def halves(x):
    high = x.astype(BF16)
    return high, (x - high.astype(F32)).astype(BF16)


def product(a, b):
    dot = functools.partial(jnp.dot, preferred_element_type=F32)
    return dot(a[0], b[0]) + (dot(a[0], b[1]) + dot(a[1], b[0]))


def stacked_product(stack, b, dims):
    dot = functools.partial(lax.dot_general, dimension_numbers=dims, preferred_element_type=F32)
    lines = stack.shape[0] // 2
    both = dot(stack, b[0])
    return both[:lines] + (both[lines:] + dot(stack[:lines], b[1]))


def kernel(
    members_hbm, a_hbm, b_hbm, innovation_hbm, weight_hbm, mask_hbm, cell_hbm,
    increment, control,
    members, innovation, obs_weight, obs_mask, obs_cell, a_all, b_all, k_hi, k_lo, at_hi, at_lo, b_hi, b_lo, stack,
    field, wfield, t_out, strip, strip_hi, strip_lo, grad, mixed, mixed_rows, grad_rows, value,
    part, got, all_parts, image, sums, box,
    load_sem, w_send, w_recv, field_send, field_recv, t_send, t_recv, x_send, x_recv, g_send, g_recv,
    part_send, part_recv, box_send, box_recv,
):
    mem_dev, levels, rows, nlon = members.shape
    parts = lax.axis_size("mem")
    strips = lax.axis_size("lat")
    per_field = strips // (mem_dev * levels)
    width = nlon // per_field
    nlat = strips * rows
    lines = mem_dev * rows
    mem = lax.axis_index("mem")
    me = lax.axis_index("lat")

    side = 4
    x, z, y, core = me // 16, me // 8 % 2, me // 2 % 4, me % 2
    column = mem * side + z * 2 + core
    plane = x * side + y
    my_member, my_part = x * 2 + z, (x + y) % per_field

    def strip_device(m, l, q):
        return m // 2 * 16 + m % 2 * 8 + (q - m // 2 + per_field) % per_field * 2 + l

    def in_column(k):
        return k // side, x * 16 + k % side // 2 * 8 + y * 2 + k % 2

    def in_plane(k):
        return mem, k // side * 16 + z * 8 + k % side * 2 + core

    loads = [
        pltpu.make_async_copy(source, target, load_sem.at[k])
        for k, (source, target) in enumerate([
            (weight_hbm, obs_weight), (mask_hbm, obs_mask), (innovation_hbm, innovation), (cell_hbm, obs_cell),
            (b_hbm, b_all), (members_hbm, members), (a_hbm, a_all),
        ])
    ]
    barrier = pltpu.get_barrier_semaphore()

    @pl.loop(1, strips)
    def _(k):
        pl.semaphore_signal(barrier, inc=1, device_id=(mem, (me + k) % strips), device_id_type=MESH)

    @pl.loop(0, parts * side)
    def _(k):
        @pl.when(k // side != mem)
        def _():
            pl.semaphore_signal(barrier, inc=1, device_id=in_column(k), device_id_type=MESH)

    for load in loads:
        load.start()
    for load in loads[:4]:
        load.wait()
    weights = obs_weight[...] * obs_mask[...].astype(F32)
    pulled = -(weights * innovation[...])
    cells = obs_cell[...]
    local = (cells // nlon) * width + cells % width
    spots = lax.broadcasted_iota(jnp.int32, (rows, levels * width), 1)
    wsum = jnp.zeros((rows, levels * width), F32)
    hsum = jnp.zeros((rows, levels * width), F32)
    for j in range(cells.shape[1]):
        hit = local[:, j : j + 1] == spots
        wsum = wsum + jnp.where(hit, weights[:, j : j + 1], 0.0)
        hsum = hsum + jnp.where(hit, pulled[:, j : j + 1], 0.0)
    for l in range(levels):
        wfield[l, mem] = wsum[:, l * width : (l + 1) * width]
        field[0, l, mem] = hsum[:, l * width : (l + 1) * width]

    pl.semaphore_wait(barrier, strips - 1 + (parts - 1) * side)

    def bytes_of(ref, sem):
        return pltpu.make_async_copy(ref, ref, sem)

    def to_column(source, target, send, recv):
        for k in range(1, parts):
            pltpu.make_async_remote_copy(
                src_ref=source,
                dst_ref=target,
                send_sem=send,
                recv_sem=recv,
                device_id=((mem + k) % parts, me),
                device_id_type=MESH,
            ).start()

    for l in range(levels):
        to_column(field.at[0, l, mem], field.at[0, l, mem], field_send.at[0, l], field_recv.at[0, l])
    loads[4].wait()
    for q in range(per_field):
        high, low = halves(b_all[:, q * width : (q + 1) * width])
        b_hi[q] = high
        b_lo[q] = low
    loads[6].wait()
    transposed = halves(a_all[...].T)
    at_hi[...], at_lo[...] = transposed
    k_hi[...], k_lo[...] = halves(product(halves(a_all[...]), transposed))
    loads[5].wait()

    def sent_strips(b, l):
        @pl.when(core == l)
        def _():
            bytes_of(strip.at[b, pl.ds(0, (strips // levels - 1) * rows)], t_send.at[b, l]).wait()

        @pl.when(core != l)
        def _():
            bytes_of(strip.at[b, pl.ds(0, strips // levels * rows)], t_send.at[b, l]).wait()

    def strips_of(b, l):
        if b == 0:
            bytes_of(field.at[0, l, pl.ds(0, parts - 1)], field_recv.at[0, l]).wait()
        for q in range(per_field):
            block = (members[:, l, :, q * width : (q + 1) * width] * field[b, l, q][None]).reshape(lines, width)
            high, low = halves(block)
            stack[:lines, q * width : (q + 1) * width] = high
            stack[lines:, q * width : (q + 1) * width] = low

        @pl.loop(0, per_field)
        def _(t):
            q = (my_part + t) % per_field
            t_out[b, l, q] = stacked_product(stack[...], (b_hi[q], b_lo[q]), NN)

            @pl.when((l > 0) & (t == 0))
            def _():
                sent_strips(b, 0)

            @pl.loop(0, mem_dev)
            def _(k):
                m = (x + 6 - k // 2) % 4 * 2 + (z + k + 1) % 2
                d = strip_device(m, l, q)

                @pl.when(d != me)
                def _():
                    pltpu.make_async_remote_copy(
                        src_ref=t_out.at[b, l, q, pl.ds(m * rows, rows)],
                        dst_ref=strip.at[b, pl.ds(me * rows, rows)],
                        send_sem=t_send.at[b, l],
                        recv_sem=t_recv.at[b],
                        device_id=(mem, d),
                        device_id_type=MESH,
                    ).start()

                @pl.when(d == me)
                def _():
                    pltpu.make_async_copy(
                        t_out.at[b, l, q, pl.ds(m * rows, rows)], strip.at[b, pl.ds(me * rows, rows)], t_recv.at[b]
                    ).start()

    def to_rows(b, source, target, send, recv, pieces):
        mine = target.at[b, core, my_part, pl.ds(my_member * rows, rows)]
        for dx, piece in zip((2, 1, 3, 0), pieces):

            def send_one(k, dx=dx):
                d = (x + dx) % 4 * 16 + (z + k // 2 + 1) % 2 * 8 + (y + 6 - k // 4) % 4 * 2 + (core + k + 1) % 2
                pltpu.make_async_remote_copy(
                    src_ref=source.at[b, pl.ds(d * rows, rows)],
                    dst_ref=mine,
                    send_sem=send.at[b],
                    recv_sem=recv.at[b, core, my_part],
                    device_id=(mem, d),
                    device_id_type=MESH,
                ).start()

            if piece is not None:
                at = pl.ds((x + dx) % 4 * 16 * rows, 16 * rows)
                source[b, at] = piece(at)
            if dx:

                @pl.loop(0, 16)
                def _(k):
                    send_one(k)
            else:

                @pl.loop(0, 16)
                def _(k):
                    @pl.when(k != 11)
                    def _():
                        send_one(k)

        pltpu.make_async_copy(source.at[b, pl.ds(me * rows, rows)], mine, recv.at[b, core, my_part]).start()

    def mix(b):
        bytes_of(strip.at[b], t_recv.at[b]).wait()
        high, low = halves(strip[b])
        strip_hi[b] = high
        strip_lo[b] = low
        to_rows(
            b, mixed, mixed_rows, x_send, x_recv,
            [lambda at: product((k_hi[at], k_lo[at]), (high, low))] * 4,
        )

    def gradient_of(b):
        grad[b] = product((at_hi[...], at_lo[...]), (strip_hi[b], strip_lo[b]))

    def send_gradient(b):
        to_rows(b, grad, grad_rows, g_send, g_recv, [None] * 4)

    def part_of(b, l):
        value[...] = jnp.zeros_like(value)

        @pl.loop(0, per_field)
        def _(q):
            bytes_of(mixed_rows.at[b, l, q], x_recv.at[b, l, q]).wait()
            value[...] += stacked_product(jnp.concatenate(halves(mixed_rows[b, l, q]), axis=0), (b_hi[q], b_lo[q]), NT)

        for q in range(parts):
            shaped = value[:, q * width : (q + 1) * width].reshape(mem_dev, rows, width)
            part[b, l, q] = jnp.sum(members[:, l, :, q * width : (q + 1) * width] * shaped, axis=0)
        if b == 0:
            to_column(part.at[0, l], all_parts.at[l, mem], part_send.at[0, l], part_recv.at[0, l])
            all_parts[l, mem] = part[0, l]
            return
        for k in range(1, parts):
            other = (mem + k) % parts
            pltpu.make_async_remote_copy(
                src_ref=part.at[b, l, other],
                dst_ref=got.at[b, l, mem],
                send_sem=part_send.at[b, l],
                recv_sem=part_recv.at[b, l],
                device_id=(other, me),
                device_id_type=MESH,
            ).start()
        got[b, l, mem] = part[b, l, mem]

    def image_of(b, l):
        if b == 0:
            bytes_of(all_parts.at[l, pl.ds(0, parts - 1)], part_recv.at[0, l]).wait()
            for q in range(parts):
                whole = jnp.sum(all_parts[l, :, q], axis=0)
                field[1, l, q] = wfield[l, q] * whole
            image[0, l] = jnp.sum(all_parts[l, :, mem], axis=0)
            return
        bytes_of(got.at[b, l, pl.ds(0, parts - 1)], part_recv.at[b, l]).wait()
        image[b, l] = jnp.sum(got[b, l], axis=0)

    def lanes(x):
        return jnp.sum(x.reshape(-1, 8, 128), axis=0).sum(axis=0, keepdims=True)

    def start_round(b, n, slot, device):
        @pl.loop(1, parts * side)
        def _(k):
            pltpu.make_async_remote_copy(
                src_ref=sums.at[b, n],
                dst_ref=box.at[b, n, slot],
                send_sem=box_send.at[b, n],
                recv_sem=box_recv.at[b, n],
                device_id=device((slot + k) % (parts * side)),
                device_id_type=MESH,
            ).start()

        box[b, n, slot] = sums[b, n]

    def end_round(b, n):
        bytes_of(box.at[b, n, pl.ds(0, parts * side - 1)], box_recv.at[b, n]).wait()
        return jnp.sum(box[b, n], axis=0)

    def start_sums(b, norm, seen):
        row = lax.broadcasted_iota(jnp.int32, (8, 128), 0)
        sums[b, 0] = jnp.where(row == 0, lanes(norm), 0.0) + jnp.where(row == 1, lanes(seen), 0.0)
        start_round(b, 0, column, in_column)

    def pass_sums(b):
        sums[b, 1] = end_round(b, 0)
        start_round(b, 1, plane, in_plane)

    def end_sums(b):
        total = end_round(b, 1)
        norm = jnp.sum(total[0:1])
        return norm / (norm + jnp.sum(total[1:2]))

    def squares(x, w=None):
        y = x * x if w is None else x * x * w
        return (y[:, :128] + y[:, 128:]).reshape(-1, 8, 128)


    @pl.loop(0, levels)
    def _(l):
        strips_of(0, l)

    to_column(wfield.at[:, mem], wfield.at[:, mem], w_send.at[0], w_recv.at[0])
    mix(0)
    gradient_of(0)
    norm = squares(grad[0])

    @pl.loop(0, levels)
    def _(l):
        part_of(0, l)

    bytes_of(mixed.at[0, pl.ds(0, (parts - 1) * levels * rows)], w_recv.at[0]).wait()

    @pl.loop(0, levels)
    def _(l):
        image_of(0, l)
        strips_of(1, l)

    flat_weights = wfield[:, mem].reshape(levels * rows, width)
    image0 = image[0]
    start_sums(0, norm, squares(image0.reshape(levels * rows, width), flat_weights))
    mix(1)
    pass_sums(0)
    gradient_of(1)
    send_gradient(0)

    @pl.loop(0, levels)
    def _(l):
        part_of(1, l)

    send_gradient(1)
    length0 = end_sums(0)
    keep = 1.0 - length0
    norm = squares(keep * grad[0] - length0 * grad[1])
    for l in range(levels):
        image_of(1, l)
    image1 = keep * image0 - length0 * image[1]
    start_sums(1, norm, squares(image1.reshape(levels * rows, width), flat_weights))
    pass_sums(1)
    length1 = end_sums(1)
    first = -(length0 + length1 * keep)
    second = length1 * length0
    increment[...] = first * image0 + second * image[1]
    for l in range(levels):
        for q in range(per_field):
            for b in range(2):
                bytes_of(grad_rows.at[b, l, q], g_recv.at[b, l, q]).wait()
            block = first * grad_rows[0, l, q] + second * grad_rows[1, l, q]
            control[:, l, :, q * width : (q + 1) * width] = block.reshape(mem_dev, rows, width)
    bytes_of(mixed.at[0, pl.ds(0, (parts - 1) * levels * rows)], w_send.at[0]).wait()
    for b in range(2):
        sent = strip.at[b, pl.ds(0, nlat - rows)]
        bytes_of(sent, x_send.at[b]).wait()
        bytes_of(sent, g_send.at[b]).wait()
        sent_strips(b, 1)
        for l in range(levels):
            if b == 0:
                bytes_of(field.at[0, l, pl.ds(0, parts - 1)], field_send.at[0, l]).wait()
                bytes_of(all_parts.at[l, pl.ds(0, parts - 1)], part_send.at[0, l]).wait()
            else:
                bytes_of(field.at[b, l, pl.ds(0, parts - 1)], part_send.at[b, l]).wait()
        for n in range(2):
            bytes_of(box.at[b, n, pl.ds(0, parts * side - 1)], box_send.at[b, n]).wait()


def solution(mesh):
    parts, strips = mesh.shape["mem"], mesh.shape["lat"]

    def per_device(members, lat_root, lon_root, innovation, obs_weight, obs_mask, obs_cell):
        mem_dev, levels, rows, nlon = members.shape
        nlat = lat_root.shape[0]
        per_field = strips // (mem_dev * levels)
        width = nlon // per_field
        lines = mem_dev * rows
        vmem = pl.BlockSpec(memory_space=pltpu.VMEM)
        whole = pl.BlockSpec(memory_space=pltpu.HBM)
        slots = innovation.shape
        pair = pltpu.SemaphoreType.DMA((2,))
        levelled = pltpu.SemaphoreType.DMA((2, levels))
        quads = pltpu.SemaphoreType.DMA((2, levels, per_field))
        scratch = [
            pltpu.VMEM(members.shape, F32),
            *[pltpu.VMEM(slots, F32)] * 2,
            *[pltpu.VMEM(slots, jnp.int32)] * 2,
            pltpu.VMEM((nlat, nlat), F32),
            pltpu.VMEM((nlon, nlon), F32),
            *[pltpu.VMEM((nlat, nlat), BF16)] * 4,
            *[pltpu.VMEM((per_field, nlon, width), BF16)] * 2,
            pltpu.VMEM((2 * lines, nlon), BF16),
            pltpu.VMEM((2, levels, parts, rows, width), F32),
            pltpu.VMEM((levels, parts, rows, width), F32),
            pltpu.VMEM((2, levels, per_field, lines, width), F32),
            pltpu.VMEM((2, nlat, width), F32),
            *[pltpu.VMEM((2, nlat, width), BF16)] * 2,
            *[pltpu.VMEM((2, nlat, width), F32)] * 2,
            *[pltpu.VMEM((2, levels, per_field, lines, width), F32)] * 2,
            pltpu.VMEM((lines, nlon), F32),
            *[pltpu.VMEM((2, levels, parts, rows, width), F32)] * 2,
            pltpu.VMEM((levels, parts, parts, rows, width), F32),
            pltpu.VMEM((2, levels, rows, width), F32),
            pltpu.VMEM((2, 2, 8, 128), F32),
            pltpu.VMEM((2, 2, 16, 8, 128), F32),
            pltpu.SemaphoreType.DMA((7,)),
            *[pltpu.SemaphoreType.DMA((1,))] * 2,
            levelled, levelled, levelled, pair,
            pair, quads, pair, quads,
            levelled, levelled,
            *[pltpu.SemaphoreType.DMA((2, 2))] * 2,
        ]
        return pl.pallas_call(
            kernel,
            out_shape=(
                jax.ShapeDtypeStruct((levels, rows, nlon // parts), F32),
                jax.ShapeDtypeStruct(members.shape, F32),
            ),
            in_specs=[whole] * 7,
            out_specs=(vmem, vmem),
            scratch_shapes=scratch,
            compiler_params=pltpu.CompilerParams(
                collective_id=0, has_side_effects=True, vmem_limit_bytes=62 * 1024 * 1024
            ),
            cost_estimate=pl.CostEstimate(flops=5_000_000_000, bytes_accessed=7_000_000, transcendentals=0),
        )(members, lat_root, lon_root, innovation, obs_weight, obs_mask, obs_cell)

    return jax.shard_map(
        per_device,
        mesh=mesh,
        in_specs=(P("mem", None, "lat", None), P(), P(), *[P("lat", "mem")] * 4),
        out_specs=(P(None, "lat", "mem"), P("mem", None, "lat", None)),
        check_vma=False,
    )
```

```python
import functools

import jax
import jax.numpy as jnp
from jax import lax
from jax.experimental import pallas as pl
from jax.experimental.pallas import tpu as pltpu
from jax.sharding import PartitionSpec as P

MESH = pl.DeviceIdType.MESH
F32 = jnp.float32
BF16 = jnp.bfloat16
NN = (((1,), (0,)), ((), ()))
NT = (((1,), (1,)), ((), ()))


def halves(x):
    high = x.astype(BF16)
    return high, (x - high.astype(F32)).astype(BF16)


def product(a, b):
    dot = functools.partial(jnp.dot, preferred_element_type=F32)
    return dot(a[0], b[0]) + (dot(a[0], b[1]) + dot(a[1], b[0]))


def stacked_product(stack, b, dims):
    dot = functools.partial(lax.dot_general, dimension_numbers=dims, preferred_element_type=F32)
    lines = stack.shape[0] // 2
    both = dot(stack, b[0])
    return both[:lines] + (both[lines:] + dot(stack[:lines], b[1]))


def kernel(
    members_hbm, a_hbm, b_hbm, innovation_hbm, weight_hbm, mask_hbm, cell_hbm,
    increment, control,
    members, innovation, obs_weight, obs_mask, obs_cell, a_all, b_all, k_hi, k_lo, at_hi, at_lo, b_hi, b_lo, stack,
    field, wfield, t_out, strip, strip_hi, strip_lo, grad, mixed, mixed_rows, grad_rows, value,
    part, got, all_parts, image, sums, box,
    load_sem, w_send, w_recv, field_send, field_recv, t_send, t_recv, x_send, x_recv, g_send, g_recv,
    part_send, part_recv, box_send, box_recv,
):
    mem_dev, levels, rows, nlon = members.shape
    parts = lax.axis_size("mem")
    strips = lax.axis_size("lat")
    per_field = strips // (mem_dev * levels)
    width = nlon // per_field
    nlat = strips * rows
    lines = mem_dev * rows
    mem = lax.axis_index("mem")
    me = lax.axis_index("lat")

    side = 4
    x, z, y, core = me // 16, me // 8 % 2, me // 2 % 4, me % 2
    column = mem * side + z * 2 + core
    plane = x * side + y
    my_member, my_part = x * 2 + z, (x + y) % per_field

    def strip_device(m, l, q):
        return m // 2 * 16 + m % 2 * 8 + (q - m // 2 + per_field) % per_field * 2 + l

    def in_column(k):
        return k // side, x * 16 + k % side // 2 * 8 + y * 2 + k % 2

    def in_plane(k):
        return mem, k // side * 16 + z * 8 + k % side * 2 + core

    loads = [
        pltpu.make_async_copy(source, target, load_sem.at[k])
        for k, (source, target) in enumerate([
            (weight_hbm, obs_weight), (mask_hbm, obs_mask), (innovation_hbm, innovation), (cell_hbm, obs_cell),
            (b_hbm, b_all), (members_hbm, members), (a_hbm, a_all),
        ])
    ]
    barrier = pltpu.get_barrier_semaphore()

    @pl.loop(1, strips)
    def _(k):
        pl.semaphore_signal(barrier, inc=1, device_id=(mem, (me + k) % strips), device_id_type=MESH)

    @pl.loop(0, parts * side)
    def _(k):
        @pl.when(k // side != mem)
        def _():
            pl.semaphore_signal(barrier, inc=1, device_id=in_column(k), device_id_type=MESH)

    for load in loads:
        load.start()
    for load in loads[:4]:
        load.wait()
    weights = obs_weight[...] * obs_mask[...].astype(F32)
    pulled = -(weights * innovation[...])
    cells = obs_cell[...]
    local = (cells // nlon) * width + cells % width
    spots = lax.broadcasted_iota(jnp.int32, (rows, levels * width), 1)
    wsum = jnp.zeros((rows, levels * width), F32)
    hsum = jnp.zeros((rows, levels * width), F32)
    for j in range(cells.shape[1]):
        hit = local[:, j : j + 1] == spots
        wsum = wsum + jnp.where(hit, weights[:, j : j + 1], 0.0)
        hsum = hsum + jnp.where(hit, pulled[:, j : j + 1], 0.0)
    for l in range(levels):
        wfield[l, mem] = wsum[:, l * width : (l + 1) * width]
        field[0, l, mem] = hsum[:, l * width : (l + 1) * width]

    pl.semaphore_wait(barrier, strips - 1 + (parts - 1) * side)

    def bytes_of(ref, sem):
        return pltpu.make_async_copy(ref, ref, sem)

    def to_column(source, target, send, recv):
        for k in range(1, parts):
            pltpu.make_async_remote_copy(
                src_ref=source,
                dst_ref=target,
                send_sem=send,
                recv_sem=recv,
                device_id=((mem + k) % parts, me),
                device_id_type=MESH,
            ).start()

    for l in range(levels):
        to_column(field.at[0, l, mem], field.at[0, l, mem], field_send.at[0, l], field_recv.at[0, l])
    loads[4].wait()
    for q in range(per_field):
        high, low = halves(b_all[:, q * width : (q + 1) * width])
        b_hi[q] = high
        b_lo[q] = low
    loads[6].wait()
    transposed = halves(a_all[...].T)
    at_hi[...], at_lo[...] = transposed
    k_hi[...], k_lo[...] = halves(product(halves(a_all[...]), transposed))
    loads[5].wait()

    def sent_strips(b, l):
        @pl.when(core == l)
        def _():
            bytes_of(strip.at[b, pl.ds(0, (strips // levels - 1) * rows)], t_send.at[b, l]).wait()

        @pl.when(core != l)
        def _():
            bytes_of(strip.at[b, pl.ds(0, strips // levels * rows)], t_send.at[b, l]).wait()

    def strips_of(b, l):
        if b == 0:
            bytes_of(field.at[0, l, pl.ds(0, parts - 1)], field_recv.at[0, l]).wait()
        for q in range(per_field):
            block = (members[:, l, :, q * width : (q + 1) * width] * field[b, l, q][None]).reshape(lines, width)
            high, low = halves(block)
            stack[:lines, q * width : (q + 1) * width] = high
            stack[lines:, q * width : (q + 1) * width] = low

        @pl.loop(0, per_field)
        def _(t):
            q = (my_part + t) % per_field
            t_out[b, l, q] = stacked_product(stack[...], (b_hi[q], b_lo[q]), NN)

            if b == 0:

                @pl.when((l > 0) & (t == 0))
                def _():
                    sent_strips(b, 0)

            @pl.loop(0, mem_dev)
            def _(k):
                m = (x + 6 - k // 2) % 4 * 2 + (z + k + 1) % 2
                d = strip_device(m, l, q)

                @pl.when(d != me)
                def _():
                    pltpu.make_async_remote_copy(
                        src_ref=t_out.at[b, l, q, pl.ds(m * rows, rows)],
                        dst_ref=strip.at[b, pl.ds(me * rows, rows)],
                        send_sem=t_send.at[b, l],
                        recv_sem=t_recv.at[b],
                        device_id=(mem, d),
                        device_id_type=MESH,
                    ).start()

                @pl.when(d == me)
                def _():
                    pltpu.make_async_copy(
                        t_out.at[b, l, q, pl.ds(m * rows, rows)], strip.at[b, pl.ds(me * rows, rows)], t_recv.at[b]
                    ).start()

    def to_rows(b, source, target, send, recv, pieces):
        mine = target.at[b, core, my_part, pl.ds(my_member * rows, rows)]
        for dx, piece in zip((2, 1, 3, 0), pieces):

            def send_one(k, dx=dx):
                d = (x + dx) % 4 * 16 + (z + k // 2 + 1) % 2 * 8 + (y + 6 - k // 4) % 4 * 2 + (core + k + 1) % 2
                pltpu.make_async_remote_copy(
                    src_ref=source.at[b, pl.ds(d * rows, rows)],
                    dst_ref=mine,
                    send_sem=send.at[b],
                    recv_sem=recv.at[b, core, my_part],
                    device_id=(mem, d),
                    device_id_type=MESH,
                ).start()

            if piece is not None:
                at = pl.ds((x + dx) % 4 * 16 * rows, 16 * rows)
                source[b, at] = piece(at)
            if dx:

                @pl.loop(0, 16)
                def _(k):
                    send_one(k)
            else:

                @pl.loop(0, 16)
                def _(k):
                    @pl.when(k != 11)
                    def _():
                        send_one(k)

        pltpu.make_async_copy(source.at[b, pl.ds(me * rows, rows)], mine, recv.at[b, core, my_part]).start()

    def mix(b):
        bytes_of(strip.at[b], t_recv.at[b]).wait()
        high, low = halves(strip[b])
        strip_hi[b] = high
        strip_lo[b] = low
        to_rows(
            b, mixed, mixed_rows, x_send, x_recv,
            [lambda at: product((k_hi[at], k_lo[at]), (high, low))] * 4,
        )

    def gradient_of(b):
        grad[b] = product((at_hi[...], at_lo[...]), (strip_hi[b], strip_lo[b]))

    def send_gradient(b):
        to_rows(b, grad, grad_rows, g_send, g_recv, [None] * 4)

    def part_of(b, l):
        value[...] = jnp.zeros_like(value)

        @pl.loop(0, per_field)
        def _(q):
            bytes_of(mixed_rows.at[b, l, q], x_recv.at[b, l, q]).wait()
            value[...] += stacked_product(jnp.concatenate(halves(mixed_rows[b, l, q]), axis=0), (b_hi[q], b_lo[q]), NT)

        for q in range(parts):
            shaped = value[:, q * width : (q + 1) * width].reshape(mem_dev, rows, width)
            part[b, l, q] = jnp.sum(members[:, l, :, q * width : (q + 1) * width] * shaped, axis=0)
        if b == 0:
            to_column(part.at[0, l], all_parts.at[l, mem], part_send.at[0, l], part_recv.at[0, l])
            all_parts[l, mem] = part[0, l]
            return
        for k in range(1, parts):
            other = (mem + k) % parts
            pltpu.make_async_remote_copy(
                src_ref=part.at[b, l, other],
                dst_ref=got.at[b, l, mem],
                send_sem=part_send.at[b, l],
                recv_sem=part_recv.at[b, l],
                device_id=(other, me),
                device_id_type=MESH,
            ).start()
        got[b, l, mem] = part[b, l, mem]

    def image_of(b, l):
        if b == 0:
            bytes_of(all_parts.at[l, pl.ds(0, parts - 1)], part_recv.at[0, l]).wait()
            for q in range(parts):
                whole = jnp.sum(all_parts[l, :, q], axis=0)
                field[1, l, q] = wfield[l, q] * whole
            image[0, l] = jnp.sum(all_parts[l, :, mem], axis=0)
            return
        bytes_of(got.at[b, l, pl.ds(0, parts - 1)], part_recv.at[b, l]).wait()
        image[b, l] = jnp.sum(got[b, l], axis=0)

    def lanes(x):
        return jnp.sum(x.reshape(-1, 8, 128), axis=0).sum(axis=0, keepdims=True)

    def start_round(b, n, slot, device):
        @pl.loop(1, parts * side)
        def _(k):
            pltpu.make_async_remote_copy(
                src_ref=sums.at[b, n],
                dst_ref=box.at[b, n, slot],
                send_sem=box_send.at[b, n],
                recv_sem=box_recv.at[b, n],
                device_id=device((slot + k) % (parts * side)),
                device_id_type=MESH,
            ).start()

        box[b, n, slot] = sums[b, n]

    def end_round(b, n):
        bytes_of(box.at[b, n, pl.ds(0, parts * side - 1)], box_recv.at[b, n]).wait()
        return jnp.sum(box[b, n], axis=0)

    def start_sums(b, norm, seen):
        row = lax.broadcasted_iota(jnp.int32, (8, 128), 0)
        sums[b, 0] = jnp.where(row == 0, lanes(norm), 0.0) + jnp.where(row == 1, lanes(seen), 0.0)
        start_round(b, 0, column, in_column)

    def pass_sums(b):
        sums[b, 1] = end_round(b, 0)
        start_round(b, 1, plane, in_plane)

    def end_sums(b):
        total = end_round(b, 1)
        norm = jnp.sum(total[0:1])
        return norm / (norm + jnp.sum(total[1:2]))

    def squares(x, w=None):
        y = x * x if w is None else x * x * w
        return (y[:, :128] + y[:, 128:]).reshape(-1, 8, 128)


    @pl.loop(0, levels)
    def _(l):
        strips_of(0, l)

    to_column(wfield.at[:, mem], wfield.at[:, mem], w_send.at[0], w_recv.at[0])
    mix(0)
    gradient_of(0)
    norm = squares(grad[0])

    @pl.loop(0, levels)
    def _(l):
        part_of(0, l)

    bytes_of(mixed.at[0, pl.ds(0, (parts - 1) * levels * rows)], w_recv.at[0]).wait()

    @pl.loop(0, levels)
    def _(l):
        image_of(0, l)
        strips_of(1, l)

    flat_weights = wfield[:, mem].reshape(levels * rows, width)
    image0 = image[0]
    start_sums(0, norm, squares(image0.reshape(levels * rows, width), flat_weights))
    mix(1)
    pass_sums(0)
    gradient_of(1)
    send_gradient(0)

    @pl.loop(0, levels)
    def _(l):
        part_of(1, l)

    send_gradient(1)
    length0 = end_sums(0)
    keep = 1.0 - length0
    norm = squares(keep * grad[0] - length0 * grad[1])
    for l in range(levels):
        image_of(1, l)
    image1 = keep * image0 - length0 * image[1]
    start_sums(1, norm, squares(image1.reshape(levels * rows, width), flat_weights))
    pass_sums(1)
    length1 = end_sums(1)
    first = -(length0 + length1 * keep)
    second = length1 * length0
    increment[...] = first * image0 + second * image[1]
    for l in range(levels):
        for q in range(per_field):
            for b in range(2):
                bytes_of(grad_rows.at[b, l, q], g_recv.at[b, l, q]).wait()
            block = first * grad_rows[0, l, q] + second * grad_rows[1, l, q]
            control[:, l, :, q * width : (q + 1) * width] = block.reshape(mem_dev, rows, width)
    bytes_of(mixed.at[0, pl.ds(0, (parts - 1) * levels * rows)], w_send.at[0]).wait()
    for b in range(2):
        sent = strip.at[b, pl.ds(0, nlat - rows)]
        bytes_of(sent, x_send.at[b]).wait()
        bytes_of(sent, g_send.at[b]).wait()
        if b == 1:
            sent_strips(b, 0)
        sent_strips(b, 1)
        for l in range(levels):
            if b == 0:
                bytes_of(field.at[0, l, pl.ds(0, parts - 1)], field_send.at[0, l]).wait()
                bytes_of(all_parts.at[l, pl.ds(0, parts - 1)], part_send.at[0, l]).wait()
            else:
                bytes_of(field.at[b, l, pl.ds(0, parts - 1)], part_send.at[b, l]).wait()
        for n in range(2):
            bytes_of(box.at[b, n, pl.ds(0, parts * side - 1)], box_send.at[b, n]).wait()


def solution(mesh):
    parts, strips = mesh.shape["mem"], mesh.shape["lat"]

    def per_device(members, lat_root, lon_root, innovation, obs_weight, obs_mask, obs_cell):
        mem_dev, levels, rows, nlon = members.shape
        nlat = lat_root.shape[0]
        per_field = strips // (mem_dev * levels)
        width = nlon // per_field
        lines = mem_dev * rows
        vmem = pl.BlockSpec(memory_space=pltpu.VMEM)
        whole = pl.BlockSpec(memory_space=pltpu.HBM)
        slots = innovation.shape
        pair = pltpu.SemaphoreType.DMA((2,))
        levelled = pltpu.SemaphoreType.DMA((2, levels))
        quads = pltpu.SemaphoreType.DMA((2, levels, per_field))
        scratch = [
            pltpu.VMEM(members.shape, F32),
            *[pltpu.VMEM(slots, F32)] * 2,
            *[pltpu.VMEM(slots, jnp.int32)] * 2,
            pltpu.VMEM((nlat, nlat), F32),
            pltpu.VMEM((nlon, nlon), F32),
            *[pltpu.VMEM((nlat, nlat), BF16)] * 4,
            *[pltpu.VMEM((per_field, nlon, width), BF16)] * 2,
            pltpu.VMEM((2 * lines, nlon), BF16),
            pltpu.VMEM((2, levels, parts, rows, width), F32),
            pltpu.VMEM((levels, parts, rows, width), F32),
            pltpu.VMEM((2, levels, per_field, lines, width), F32),
            pltpu.VMEM((2, nlat, width), F32),
            *[pltpu.VMEM((2, nlat, width), BF16)] * 2,
            *[pltpu.VMEM((2, nlat, width), F32)] * 2,
            *[pltpu.VMEM((2, levels, per_field, lines, width), F32)] * 2,
            pltpu.VMEM((lines, nlon), F32),
            *[pltpu.VMEM((2, levels, parts, rows, width), F32)] * 2,
            pltpu.VMEM((levels, parts, parts, rows, width), F32),
            pltpu.VMEM((2, levels, rows, width), F32),
            pltpu.VMEM((2, 2, 8, 128), F32),
            pltpu.VMEM((2, 2, 16, 8, 128), F32),
            pltpu.SemaphoreType.DMA((7,)),
            *[pltpu.SemaphoreType.DMA((1,))] * 2,
            levelled, levelled, levelled, pair,
            pair, quads, pair, quads,
            levelled, levelled,
            *[pltpu.SemaphoreType.DMA((2, 2))] * 2,
        ]
        return pl.pallas_call(
            kernel,
            out_shape=(
                jax.ShapeDtypeStruct((levels, rows, nlon // parts), F32),
                jax.ShapeDtypeStruct(members.shape, F32),
            ),
            in_specs=[whole] * 7,
            out_specs=(vmem, vmem),
            scratch_shapes=scratch,
            compiler_params=pltpu.CompilerParams(
                collective_id=0, has_side_effects=True, vmem_limit_bytes=62 * 1024 * 1024
            ),
            cost_estimate=pl.CostEstimate(flops=5_000_000_000, bytes_accessed=7_000_000, transcendentals=0),
        )(members, lat_root, lon_root, innovation, obs_weight, obs_mask, obs_cell)

    return jax.shard_map(
        per_device,
        mesh=mesh,
        in_specs=(P("mem", None, "lat", None), P(), P(), *[P("lat", "mem")] * 4),
        out_specs=(P(None, "lat", "mem"), P("mem", None, "lat", None)),
        check_vma=False,
    )
```
